32 devices in a mesh: groups: 2 (over y), ep: 16 (over z, x, core), tp: 1.
Axes of the slice: x: 2, y: 2, z: 4, core: 2. Of those that a mesh axis runs over, the one named last changes fastest.
Arguments:
- tokens: bfloat16 [128, 3584], P(('groups', 'ep')), parts along dimension 0, may hold values from -6 to 6
- routes: int32 [128, 8], P(('groups', 'ep')), parts along dimension 0, may hold values from 0 to 15, all different within a row; in each aligned block of 4 rows (0 to 3, 4 to 7, ...) at most 2 rows name the same one
- route_weights: bfloat16 [128, 8], P(('groups', 'ep')), parts along dimension 0, may hold values from 0.049804688 to 1
- gate_codes: bfloat16 [3584, 32768], P(None, ('ep', 'tp')), may hold values from -8 to 7, as said below
- gate_scales: float32 [28, 32768], P(None, ('ep', 'tp')), may hold values from 0.002 to 0.006
- up_codes: bfloat16 [3584, 32768], P(None, ('ep', 'tp')), may hold values from -8 to 7, as said below
- up_scales: float32 [28, 32768], P(None, ('ep', 'tp')), may hold values from 0.002 to 0.006
- down_codes: bfloat16 [32768, 3584], P(('ep', 'tp')), may hold values from -8 to 7, as said below
- down_scales: float32 [256, 3584], P(('ep', 'tp')), may hold values from 0.003 to 0.008
Outputs:
- mixed: bfloat16 [128, 3584], P(('groups', 'ep'), 'tp'), parts along dimension 0
- hessian: float32 [65536, 2048], P(('groups', 'ep', 'tp')), parts along dimension 0
The draws below stay inside these ranges and needn't reach their ends.
There are 2 independent parts, one for each index of `groups`. The reference program is written for one: setup_inputs(seed, part) draws one part's arguments, and reference() takes and returns one part's arrays. A program takes and returns all parts, laid end to end along the dimension named above; an argument that names none is the same for every part. Nothing has to cross between parts.
Inputs may be any that keep to these rules, and one draw needn't show every extreme that they name: `routes`: each row names 8 different experts. Among the rows of one index of ep no expert is named more than 2 times, a bound that some block reaches. `gate_codes`: integer values. `up_codes`: integer values. `down_codes`: integer values.
All inputs are finite; a program needn't handle non-finite values.
Results may differ from the reference program's by a relative error of at most 0.0072.
Values may be sent and summed in bfloat16 or wider, within the bound.
A program may use at most 128 MiB of HBM per device.

```python
import math
import jax
import jax.numpy as jnp
import numpy as np
from jax import lax

D = 3584
FF = 2048
TOP = 8
GROUP = 128
TOK_DEV = 4
EXPERTS = 16
CAP = 2
FF_DEV = 2048
HBLOCK = 2048
TOKENS = 64


def draw_gate_codes(key, part):
    key = jax.random.fold_in(key, 11)
    return jax.random.randint(key, (D, EXPERTS * FF), -8, 8).astype(jnp.float32).astype(jnp.bfloat16)


def draw_up_codes(key, part):
    key = jax.random.fold_in(key, 12)
    return jax.random.randint(key, (D, EXPERTS * FF), -8, 8).astype(jnp.float32).astype(jnp.bfloat16)


def draw_down_codes(key, part):
    key = jax.random.fold_in(key, 13)
    return jax.random.randint(key, (EXPERTS * FF, D), -8, 8).astype(jnp.float32).astype(jnp.bfloat16)


def steps_of(own_key, extent, shards, low, largest):
    factor_of = 1.0
    for position, shards_of in shards:
        steps = jax.random.uniform(jax.random.fold_in(jax.random.fold_in(own_key, 6), position), (shards_of,), jnp.float32, low / len(shards), largest / len(shards))
        factor_of = factor_of * jnp.repeat(jnp.exp(steps), extent[position] // shards_of).reshape((-1,) + (1,) * (len(extent) - 1 - position))
    return factor_of


def assign_block(key, own, number, rows, amount, top, limit, skew):
    ranking = jax.random.permutation(key, amount)
    crowded, ordinary = portions_of(amount, rows * top, limit, skew, True), portions_of(amount, rows * top, limit, skew, False)
    places = jnp.arange(amount)

    def named(lengths, offset_by):
        used = int((lengths > 0).sum())
        fixed = max(1, used // 4)
        shifted = fixed + (places - fixed + offset_by * (used - fixed)) % max(1, amount - fixed)
        return jnp.zeros((amount,), jnp.int32).at[ranking[jnp.where(places < fixed, places, shifted)]].set(jnp.asarray(lengths, jnp.int32))

    lengths = jnp.where(number % 4 == 0, named(crowded, number // 4), named(ordinary, number - number // 4 - 1))
    mixed = jax.random.permutation(jax.random.fold_in(own, 3), amount)
    giver, sink = mixed[0:amount // 2 * 2:2], mixed[1:amount // 2 * 2:2]
    slack = jnp.minimum(lengths[giver] - 1, limit - lengths[sink]) // 2
    slack = jnp.where((giver == ranking[0]) | (sink == ranking[0]) | (lengths[sink] == 0), 0, jnp.maximum(slack, 0))
    shifted = jax.random.randint(jax.random.fold_in(own, 4), (amount // 2,), 0, 1 << 20) % (slack + 1)
    lengths = lengths.at[giver].add(-shifted).at[sink].add(shifted)
    members = jnp.searchsorted(jnp.cumsum(lengths), jnp.arange(rows * top), side="right").astype(jnp.int32)
    table = members.reshape(top, rows).T
    table = table[jax.random.permutation(jax.random.fold_in(own, 1), rows)]
    offset_by = jax.random.randint(jax.random.fold_in(own, 2), (rows, 1), 0, top)
    return jnp.take_along_axis(table, (jnp.arange(top)[None, :] + offset_by) % top, axis=1)


def portions_of(number_of, total, most, lean, full):
    loads = [(1 << 20) // math.isqrt(standing ** lean) + 1 for standing in range(1, number_of + 1)]
    largest = most if full else min(most, max(-(-total // number_of), total * loads[0] // sum(loads)))
    least = 1 if total - largest >= number_of - 1 else 0
    given, surplus = [largest] + [least] * (number_of - 1), total - largest - least * (number_of - 1)
    while surplus > 0:
        free = [i for i in range(1, number_of) if given[i] < largest] or [i for i in range(1, number_of) if given[i] < most]
        whole, budget = sum([loads[i] for i in free]), surplus
        for i in free:
            addition = min(most - given[i], max(1, budget * loads[i] // whole), surplus)
            given[i] = given[i] + addition
            surplus = surplus - addition
    return np.array(given)


def bell_draw(key, shape, width, reach, cuts=(), kind=jnp.bfloat16):
    result = width * jax.random.normal(key, shape, jnp.float32)
    if cuts:
        result = result * steps_of(key, shape, cuts, -0.22, 0.18)
    return jnp.clip(result, -reach, reach).astype(kind)


def setup_inputs(seed: int = 0, part: int = 0) -> dict:
    arg_keys = jax.random.split(jax.random.key(seed), 10)
    own_keys = jax.random.split(jax.random.fold_in(arg_keys[9], part), 10)
    tokens = bell_draw(own_keys[0], (TOKENS, D), 1.0, 6.0, ((0, 16),))
    routes_keys = jax.random.split(jax.random.fold_in(own_keys[1], 1), TOKENS // TOK_DEV)
    routes_turns = jax.random.permutation(jax.random.fold_in(own_keys[1], 3), TOKENS // TOK_DEV)
    routes = jax.vmap(lambda own, number: assign_block(jax.random.fold_in(own_keys[1], 2), own, number, TOK_DEV, EXPERTS, TOP, CAP, 2))(routes_keys, routes_turns).reshape((TOKENS, TOP))
    route_weights = jnp.clip(jnp.exp(math.log(1.0) - 2.9996462 * jax.random.uniform(own_keys[2], (TOKENS, TOP), jnp.float32) ** steps_of(own_keys[2], (TOKENS, TOP), ((0, 16),), -0.2, 0.2)), 0.049804688, 1.0).astype(jnp.bfloat16)
    gate_codes = draw_gate_codes(jax.random.fold_in(arg_keys[9], 71), part)
    gate_scales = jnp.clip(jnp.exp(math.log(0.006) - 1.09861225 * jax.random.uniform(arg_keys[4], (D // GROUP, EXPERTS * FF), jnp.float32) ** steps_of(arg_keys[4], (D // GROUP, EXPERTS * FF), ((1, 16),), -0.2, 0.2)), 0.002, 0.006)
    up_codes = draw_up_codes(jax.random.fold_in(arg_keys[9], 71), part)
    up_scales = jnp.clip(jnp.exp(math.log(0.006) - 1.09861225 * jax.random.uniform(arg_keys[6], (D // GROUP, EXPERTS * FF), jnp.float32) ** steps_of(arg_keys[6], (D // GROUP, EXPERTS * FF), ((1, 16),), -0.2, 0.2)), 0.002, 0.006)
    down_codes = draw_down_codes(jax.random.fold_in(arg_keys[9], 71), part)
    down_scales = jnp.clip(jnp.exp(math.log(0.008) - 0.9808293 * jax.random.uniform(arg_keys[8], (EXPERTS * FF // GROUP, D), jnp.float32) ** steps_of(arg_keys[8], (EXPERTS * FF // GROUP, D), ((0, 16),), -0.2, 0.2)), 0.003, 0.008)
    return dict(tokens=tokens, routes=routes, route_weights=route_weights, gate_codes=gate_codes, gate_scales=gate_scales, up_codes=up_codes, up_scales=up_scales, down_codes=down_codes, down_scales=down_scales)


def dequantize(codes, scales):
    height, across = codes.shape
    blocks = codes.astype(jnp.float32).reshape(height // GROUP, GROUP, across) * scales[:, None, :]
    return blocks.reshape(height, across).astype(jnp.bfloat16)


def reference(tokens, routes, route_weights, gate_codes, gate_scales, up_codes, up_scales, down_codes, down_scales):
    gate_weight = dequantize(gate_codes, gate_scales)
    up_weight = dequantize(up_codes, up_scales)
    down_weight = dequantize(down_codes, down_scales)
    weights = route_weights.astype(jnp.float32)
    slices = FF // FF_DEV
    blocks = FF // HBLOCK

    def expert_step(total, expert):
        gate_part = lax.dynamic_slice_in_dim(gate_weight, expert * FF, FF, 1)
        up_part = lax.dynamic_slice_in_dim(up_weight, expert * FF, FF, 1)
        down_part = lax.dynamic_slice_in_dim(down_weight, expert * FF, FF, 0)
        chosen = routes == expert
        factor = jnp.sum(jnp.where(chosen, weights, jnp.float32(0.0)), axis=1)
        member = jnp.any(chosen, axis=1).astype(jnp.float32)
        gate = jnp.dot(tokens, gate_part, preferred_element_type=jnp.float32)
        up = jnp.dot(tokens, up_part, preferred_element_type=jnp.float32)
        hidden = (jax.nn.silu(gate) * up * member[:, None]).astype(jnp.bfloat16)
        wide = hidden.astype(jnp.float32)
        grouped = wide.reshape(TOKENS, blocks, HBLOCK)
        block_hess = jnp.einsum("tbi,tbj->bij", grouped, grouped) * (2.0 / TOKENS)
        sliced = wide.reshape(TOKENS, slices, FF_DEV)
        down_blocks = down_part.astype(jnp.float32).reshape(slices, FF_DEV, D)
        parts = jnp.einsum("tsi,sid->tsd", sliced, down_blocks)
        rounded = lax.optimization_barrier(parts.astype(jnp.bfloat16)).astype(jnp.float32)
        contrib = jnp.sum(rounded, axis=1)
        return total + factor[:, None] * contrib, block_hess.reshape(FF, HBLOCK)

    start = jnp.zeros((TOKENS, D), jnp.float32)
    total, hess = lax.scan(expert_step, start, jnp.arange(EXPERTS, dtype=jnp.int32))
    return total.astype(jnp.bfloat16), hess.reshape(EXPERTS * FF, HBLOCK)
```

```python
import functools

import jax
import jax.numpy as jnp
from jax import lax
from jax.experimental import pallas as pl
from jax.experimental.pallas import tpu as pltpu
from jax.sharding import PartitionSpec as P

FF = 2048
GROUP = 128


def dequantize(codes, scales):
    height, across = codes.shape
    blocks = codes.astype(jnp.float32).reshape(height // GROUP, GROUP, across) * scales[:, None, :]
    return blocks.reshape(height, across).astype(jnp.bfloat16)


def slot_targets(flat, experts, capacity):
    table = (flat[..., None] == jnp.arange(experts, dtype=jnp.int32)).astype(jnp.int32)
    earlier = jnp.cumsum(table, axis=-2) - table
    return flat * capacity + jnp.sum(earlier * table, axis=-1)


def pack_rows(tokens, targets, places, choose):
    count = places.shape[0]
    select = (targets[None, :] == places[:, None]).astype(jnp.bfloat16)
    select = select.reshape(count, tokens.shape[0], choose).sum(axis=2)
    return jnp.dot(select, tokens, preferred_element_type=jnp.float32).astype(jnp.bfloat16)


def body(
    tokens,
    routes,
    route_weights,
    gate_codes,
    gate_scales,
    up_codes,
    up_scales,
    down_codes,
    down_scales,
):
    ep_size = lax.axis_size("ep")
    tp_size = lax.axis_size("tp")
    rows, width = tokens.shape
    choose = routes.shape[1]
    unit_count = gate_codes.shape[1]
    sharing = FF // (tp_size * unit_count)
    experts = ep_size // sharing
    capacity = min(rows, rows * choose // experts + 2 * (rows // 8))
    w_gate = dequantize(gate_codes, gate_scales)
    w_up = dequantize(up_codes, up_scales)
    w_down = dequantize(down_codes, down_scales)
    targets = slot_targets(routes.reshape(-1), experts, capacity)
    places = jnp.arange(experts * capacity, dtype=jnp.int32)
    packed = pack_rows(tokens, targets, places, choose).reshape(experts, 1, capacity, width)
    packed = jnp.broadcast_to(packed, (experts, sharing, capacity, width)).reshape(
        ep_size, capacity, width
    )
    arrived = lax.all_to_all(packed, "ep", split_axis=0, concat_axis=0, tiled=True)
    rows_in = arrived.reshape(ep_size * capacity, width)
    gate = jnp.dot(rows_in, w_gate, preferred_element_type=jnp.float32)
    up = jnp.dot(rows_in, w_up, preferred_element_type=jnp.float32)
    hidden = (jax.nn.silu(gate) * up).astype(jnp.bfloat16)
    paired = lax.all_gather(hidden, "tp", axis=1, tiled=True)
    hessian = lax.dot_general(
        hidden, paired, (((0,), (0,)), ((), ())), preferred_element_type=jnp.float32
    ) * (2.0 / (rows * ep_size))
    partial_value = jnp.dot(hidden, w_down, preferred_element_type=jnp.float32).astype(jnp.bfloat16)
    returned = lax.all_to_all(
        partial_value.reshape(ep_size, capacity, width),
        "ep",
        split_axis=0,
        concat_axis=0,
        tiled=True,
    )
    slots = jnp.arange(experts * capacity, dtype=jnp.int32)
    spread = (targets[:, None] == slots[None, :]).astype(jnp.float32) * route_weights.reshape(
        -1
    ).astype(jnp.float32)[:, None]
    spread = (
        spread.reshape(rows, choose, experts * capacity)
        .sum(axis=1)
        .reshape(rows, experts, 1, capacity)
    )
    spread = jnp.broadcast_to(spread, (rows, experts, sharing, capacity)).reshape(
        rows, ep_size * capacity
    )
    combined = jnp.dot(
        spread.astype(jnp.bfloat16),
        returned.reshape(ep_size * capacity, width),
        preferred_element_type=jnp.float32,
    )
    mixed = lax.psum_scatter(combined, "tp", scatter_dimension=1, tiled=True).astype(jnp.bfloat16)
    return (mixed, hessian)


STAGE = 512
WIDE = 256
PAIR = 2 * GROUP


def pieces(total, parts):
    parts = min(parts, total)
    counts = [total // parts + (1 if i < total % parts else 0) for i in range(parts)]
    return [(sum(counts[:i]), counts[i]) for i in range(parts)]


def moe_kernel(
    plan,
    tokens,
    routes,
    route_weights,
    gate_codes,
    gate_scales,
    up_codes,
    up_scales,
    down_codes,
    down_scales,
    mixed,
    hidden_out,
    gate_v,
    up_v,
    down_v,
    gate_s,
    up_s,
    down_s,
    gate_acc,
    up_acc,
    lhs,
    lhs_down,
    *rest,
):
    ep_size, slots, out_parts, back_parts = plan
    nd, nb = len(out_parts), len(back_parts)
    sends, recvs = rest[:nd], rest[nd : 2 * nd]
    psends, precvs = rest[2 * nd : 2 * nd + nb], rest[2 * nd + nb : 2 * nd + 2 * nb]
    scale_sem, gate_sem, up_sem, down_sem, out_send, out_recv, back_send, back_recv = rest[2 * nd + 2 * nb :]
    me = lax.axis_index("ep")
    width, units = gate_v.shape
    rows = ep_size * slots
    toks = tokens.shape[0]
    stages = width // STAGE
    downs = down_v.shape[1] // STAGE

    def peer(off):
        return {"ep": lax.rem(me + off, ep_size)}

    barrier = pltpu.get_barrier_semaphore()
    for off in range(1, ep_size):
        pl.semaphore_signal(barrier, inc=1, device_id=peer(off), device_id_type=pl.DeviceIdType.MESH)

    scale_loads = [
        pltpu.make_async_copy(gate_scales, gate_s, scale_sem.at[0]),
        pltpu.make_async_copy(up_scales, up_s, scale_sem.at[1]),
        pltpu.make_async_copy(down_scales, down_s, scale_sem.at[2]),
    ]
    gate_loads, up_loads, down_loads = [], [], []
    for st in range(stages):
        part = pl.ds(st * STAGE, STAGE)
        gate_loads.append(pltpu.make_async_copy(gate_codes.at[part], gate_v.at[part], gate_sem.at[st]))
        up_loads.append(pltpu.make_async_copy(up_codes.at[part], up_v.at[part], up_sem.at[st]))
    for st in range(downs):
        part = pl.ds(st * STAGE, STAGE)
        down_loads.append(pltpu.make_async_copy(down_codes.at[:, part], down_v.at[:, part], down_sem.at[st]))
    scale_loads[0].start()
    scale_loads[1].start()
    for st in range(stages):
        gate_loads[st].start()
        up_loads[st].start()
    scale_loads[2].start()
    for load in down_loads:
        load.start()

    row = lax.broadcasted_iota(jnp.int32, (rows, routes.shape[1]), 0)
    expert = lax.rem(me + row // slots, ep_size)
    slot = (row - (row // slots) * slots)[:, :1].astype(jnp.float32)
    seen = jnp.zeros((rows, 1), jnp.float32)
    chosen, factors = [], []
    for t in range(toks):
        hit = (routes[t : t + 1, :] == expert).astype(jnp.float32)
        named = jnp.sum(hit, axis=1, keepdims=True)
        take = named * (seen == slot).astype(jnp.float32)
        weight = jnp.sum(hit * route_weights[t : t + 1, :].astype(jnp.float32), axis=1, keepdims=True)
        chosen.append(take)
        factors.append(take * weight)
        seen = seen + named

    for c, (first, count) in enumerate(out_parts):
        for st in range(count):
            lo = (first + st) * STAGE
            value = chosen[0] * tokens[0:1, lo : lo + STAGE].astype(jnp.float32)
            for t in range(1, toks):
                value = value + chosen[t] * tokens[t : t + 1, lo : lo + STAGE].astype(jnp.float32)
            value = value.reshape(ep_size, slots, STAGE).astype(jnp.bfloat16)
            sends[c][:, :, st * STAGE : (st + 1) * STAGE] = value

    pl.semaphore_wait(barrier, ep_size - 1)

    def exchange(source, target, send_sem, recv_sem, c, sign):
        copies = []
        for off in range(1, ep_size):
            copies.append(
                pltpu.make_async_remote_copy(
                    src_ref=source.at[off],
                    dst_ref=target.at[off],
                    send_sem=send_sem.at[c, off],
                    recv_sem=recv_sem.at[c, off],
                    device_id=peer(off if sign > 0 else ep_size - off),
                    device_id_type=pl.DeviceIdType.MESH,
                )
            )
        for copy in copies:
            copy.start()
        return copies

    moves = [exchange(sends[c], recvs[c], out_send, out_recv, c, 1) for c in range(nd)]

    lhs[...] = jnp.zeros_like(lhs)
    lhs_down[...] = jnp.zeros_like(lhs_down)
    scale_loads[0].wait()
    scale_loads[1].wait()

    for c, (first, count) in enumerate(out_parts):
        recvs[c][0] = sends[c][0]
        for copy in moves[c]:
            copy.wait_recv()
        for st in range(first, first + count):
            block = recvs[c][:, :, (st - first) * STAGE : (st - first + 1) * STAGE]
            block = block.astype(jnp.float32).reshape(rows, STAGE).astype(jnp.bfloat16)
            pairs = STAGE // PAIR
            for p in range(pairs):
                lhs[st * pairs + p, :rows, :GROUP] = block[:, p * PAIR : p * PAIR + GROUP]
                lhs[st * pairs + p, rows:, GROUP:] = block[:, p * PAIR + GROUP : (p + 1) * PAIR]
            gate_loads[st].wait()
            up_loads[st].wait()

            def columns(n, _, st=st, pairs=pairs):
                cols = pl.ds(pl.multiple_of(n * WIDE, WIDE), WIDE)
                for codes, scales, acc in ((gate_v, gate_s, gate_acc), (up_v, up_s, up_acc)):
                    total = None if st == 0 else acc[:, cols]
                    for p in range(pairs):
                        at = st * pairs + p
                        got = jnp.dot(
                            lhs[at], codes[at * PAIR : (at + 1) * PAIR, cols], preferred_element_type=jnp.float32
                        )
                        term = got[:rows] * scales[2 * at : 2 * at + 1, cols]
                        term = term + got[rows:] * scales[2 * at + 1 : 2 * at + 2, cols]
                        total = term if total is None else total + term
                    acc[:, cols] = total
                return 0

            lax.fori_loop(0, units // WIDE, columns, 0)

    for p in range(units // PAIR):
        gate = gate_acc[:, p * PAIR : (p + 1) * PAIR]
        up = up_acc[:, p * PAIR : (p + 1) * PAIR]
        value = (jax.nn.silu(gate) * up).astype(jnp.bfloat16)
        hidden_out[:, p * PAIR : (p + 1) * PAIR] = value
        lhs_down[p, :rows, :GROUP] = value[:, :GROUP]
        lhs_down[p, rows:, GROUP:] = value[:, GROUP:]

    scale_loads[2].wait()
    backs = []
    for c, (first, count) in enumerate(back_parts):
        for st in range(first, first + count):
            down_loads[st].wait()
            for n in range(STAGE // WIDE):
                lo = st * STAGE + n * WIDE
                total = None
                for at in range(units // PAIR):
                    got = jnp.dot(
                        lhs_down[at],
                        down_v[at * PAIR : (at + 1) * PAIR, lo : lo + WIDE],
                        preferred_element_type=jnp.float32,
                    )
                    term = got[:rows] * down_s[2 * at : 2 * at + 1, lo : lo + WIDE]
                    term = term + got[rows:] * down_s[2 * at + 1 : 2 * at + 2, lo : lo + WIDE]
                    total = term if total is None else total + term
                here = lo - first * STAGE
                psends[c][:, :, here : here + WIDE] = total.reshape(ep_size, slots, WIDE).astype(jnp.bfloat16)
        backs.append(exchange(psends[c], precvs[c], back_send, back_recv, c, -1))

    for c, (first, count) in enumerate(back_parts):
        precvs[c][0] = psends[c][0]
        for copy in backs[c]:
            copy.wait_recv()
        for st in range(count):
            value = precvs[c][:, :, st * STAGE : (st + 1) * STAGE].astype(jnp.float32).reshape(rows, STAGE)
            lo = (first + st) * STAGE
            for t in range(toks):
                total = jnp.sum(value * factors[t], axis=0, keepdims=True)
                mixed[t : t + 1, lo : lo + STAGE] = total.astype(jnp.bfloat16)

    for copies in moves + backs:
        for copy in copies:
            copy.wait_send()


def hessian_kernel(factor, left, right, out):
    out[...] = (
        lax.dot_general(left[...], right[...], (((0,), (0,)), ((), ())), preferred_element_type=jnp.float32) * factor
    )


def fused_body(*args):
    tokens, routes, route_weights, gate_codes, gate_scales, up_codes, up_scales, down_codes, down_scales = args
    ep_size = lax.axis_size("ep")
    toks, width = tokens.shape
    units = gate_codes.shape[1]
    slots = toks * routes.shape[1] // ep_size
    rows = ep_size * slots
    out_parts = pieces(width // STAGE, 2)
    back_parts = pieces(width // STAGE, 3)
    nd, nb = len(out_parts), len(back_parts)
    slabs = [pltpu.VMEM((ep_size, slots, count * STAGE), jnp.bfloat16) for _, count in out_parts]
    back_slabs = [pltpu.VMEM((ep_size, slots, count * STAGE), jnp.bfloat16) for _, count in back_parts]
    stages = width // STAGE
    whole = pl.BlockSpec(memory_space=pltpu.VMEM)
    far = pl.BlockSpec(memory_space=pl.ANY)
    mixed, hidden = pl.pallas_call(
        functools.partial(moe_kernel, (ep_size, slots, out_parts, back_parts)),
        out_shape=(
            jax.ShapeDtypeStruct((toks, width), jnp.bfloat16),
            jax.ShapeDtypeStruct((rows, units), jnp.bfloat16),
        ),
        in_specs=[whole] * 3 + [far] * 6,
        out_specs=(whole, whole),
        scratch_shapes=[
            pltpu.VMEM(gate_codes.shape, jnp.bfloat16),
            pltpu.VMEM(up_codes.shape, jnp.bfloat16),
            pltpu.VMEM(down_codes.shape, jnp.bfloat16),
            pltpu.VMEM(gate_scales.shape, jnp.float32),
            pltpu.VMEM(up_scales.shape, jnp.float32),
            pltpu.VMEM(down_scales.shape, jnp.float32),
            pltpu.VMEM((rows, units), jnp.float32),
            pltpu.VMEM((rows, units), jnp.float32),
            pltpu.VMEM((width // PAIR, 2 * rows, PAIR), jnp.bfloat16),
            pltpu.VMEM((units // PAIR, 2 * rows, PAIR), jnp.bfloat16),
            *slabs,
            *slabs,
            *back_slabs,
            *back_slabs,
            pltpu.SemaphoreType.DMA((3,)),
            pltpu.SemaphoreType.DMA((stages,)),
            pltpu.SemaphoreType.DMA((stages,)),
            pltpu.SemaphoreType.DMA((stages,)),
            pltpu.SemaphoreType.DMA((nd, ep_size)),
            pltpu.SemaphoreType.DMA((nd, ep_size)),
            pltpu.SemaphoreType.DMA((nb, ep_size)),
            pltpu.SemaphoreType.DMA((nb, ep_size)),
        ],
        compiler_params=pltpu.CompilerParams(
            collective_id=0, has_side_effects=True, vmem_limit_bytes=58 * 2**20
        ),
        name="moe",
    )(tokens, routes, route_weights, gate_codes, gate_scales, up_codes, up_scales, down_codes, down_scales)
    block = 256
    hessian = pl.pallas_call(
        functools.partial(hessian_kernel, 2.0 / (toks * ep_size)),
        out_shape=jax.ShapeDtypeStruct((units, units), jnp.float32),
        grid=(units // block,),
        in_specs=[
            pl.BlockSpec((rows, block), lambda i: (0, i)),
            pl.BlockSpec((rows, units), lambda i: (0, 0)),
        ],
        out_specs=pl.BlockSpec((block, units), lambda i: (i, 0)),
        compiler_params=pltpu.CompilerParams(vmem_limit_bytes=32 * 2**20),
        name="hessian",
    )(hidden, hidden)
    return (mixed, hessian)


def fits(mesh, tokens, routes, gate_codes, down_codes):
    ep_size = mesh.shape["ep"]
    toks = tokens.shape[0] // (mesh.shape["groups"] * ep_size)
    units = gate_codes.shape[1] // (ep_size * mesh.shape["tp"])
    asked = toks * routes.shape[1]
    rows_limit = min(toks, asked // ep_size + 2 * (toks // 8))
    return (
        mesh.shape["tp"] == 1
        and units == FF
        and asked == ep_size * rows_limit
        and tokens.shape[1] % STAGE == 0
        and units % STAGE == 0
    )


def solution(mesh):
    placed = (
        P(("groups", "ep"), None),
        P(("groups", "ep"), None),
        P(("groups", "ep"), None),
        P(None, ("ep", "tp")),
        P(None, ("ep", "tp")),
        P(None, ("ep", "tp")),
        P(None, ("ep", "tp")),
        P(("ep", "tp"), None),
        P(("ep", "tp"), None),
    )

    def run(*args):
        fused = fits(mesh, args[0], args[1], args[3], args[7])
        return jax.shard_map(
            fused_body if fused else body,
            mesh=mesh,
            in_specs=placed,
            out_specs=(P(("groups", "ep"), "tp"), P(("groups", "ep", "tp"), None)),
            check_vma=False,
        )(*args)

    return run
```

```python
import functools
import math

import jax
import jax.numpy as jnp
from jax import lax
from jax.experimental import pallas as pl
from jax.experimental.pallas import tpu as pltpu
from jax.sharding import PartitionSpec as P

FF = 2048
GROUP = 128


def dequantize(codes, scales):
    height, across = codes.shape
    blocks = codes.astype(jnp.float32).reshape(height // GROUP, GROUP, across) * scales[:, None, :]
    return blocks.reshape(height, across).astype(jnp.bfloat16)


def slot_targets(flat, experts, capacity):
    table = (flat[..., None] == jnp.arange(experts, dtype=jnp.int32)).astype(jnp.int32)
    earlier = jnp.cumsum(table, axis=-2) - table
    return flat * capacity + jnp.sum(earlier * table, axis=-1)


def pack_rows(tokens, targets, places, choose):
    count = places.shape[0]
    select = (targets[None, :] == places[:, None]).astype(jnp.bfloat16)
    select = select.reshape(count, tokens.shape[0], choose).sum(axis=2)
    return jnp.dot(select, tokens, preferred_element_type=jnp.float32).astype(jnp.bfloat16)


def body(
    tokens,
    routes,
    route_weights,
    gate_codes,
    gate_scales,
    up_codes,
    up_scales,
    down_codes,
    down_scales,
):
    ep_size = lax.axis_size("ep")
    tp_size = lax.axis_size("tp")
    rows, width = tokens.shape
    choose = routes.shape[1]
    unit_count = gate_codes.shape[1]
    sharing = FF // (tp_size * unit_count)
    experts = ep_size // sharing
    capacity = min(rows, rows * choose // experts + 2 * (rows // 8))
    w_gate = dequantize(gate_codes, gate_scales)
    w_up = dequantize(up_codes, up_scales)
    w_down = dequantize(down_codes, down_scales)
    targets = slot_targets(routes.reshape(-1), experts, capacity)
    places = jnp.arange(experts * capacity, dtype=jnp.int32)
    packed = pack_rows(tokens, targets, places, choose).reshape(experts, 1, capacity, width)
    packed = jnp.broadcast_to(packed, (experts, sharing, capacity, width)).reshape(
        ep_size, capacity, width
    )
    arrived = lax.all_to_all(packed, "ep", split_axis=0, concat_axis=0, tiled=True)
    rows_in = arrived.reshape(ep_size * capacity, width)
    gate = jnp.dot(rows_in, w_gate, preferred_element_type=jnp.float32)
    up = jnp.dot(rows_in, w_up, preferred_element_type=jnp.float32)
    hidden = (jax.nn.silu(gate) * up).astype(jnp.bfloat16)
    paired = lax.all_gather(hidden, "tp", axis=1, tiled=True)
    hessian = lax.dot_general(
        hidden, paired, (((0,), (0,)), ((), ())), preferred_element_type=jnp.float32
    ) * (2.0 / (rows * ep_size))
    partial_value = jnp.dot(hidden, w_down, preferred_element_type=jnp.float32).astype(jnp.bfloat16)
    returned = lax.all_to_all(
        partial_value.reshape(ep_size, capacity, width),
        "ep",
        split_axis=0,
        concat_axis=0,
        tiled=True,
    )
    slots = jnp.arange(experts * capacity, dtype=jnp.int32)
    spread = (targets[:, None] == slots[None, :]).astype(jnp.float32) * route_weights.reshape(
        -1
    ).astype(jnp.float32)[:, None]
    spread = (
        spread.reshape(rows, choose, experts * capacity)
        .sum(axis=1)
        .reshape(rows, experts, 1, capacity)
    )
    spread = jnp.broadcast_to(spread, (rows, experts, sharing, capacity)).reshape(
        rows, ep_size * capacity
    )
    combined = jnp.dot(
        spread.astype(jnp.bfloat16),
        returned.reshape(ep_size * capacity, width),
        preferred_element_type=jnp.float32,
    )
    mixed = lax.psum_scatter(combined, "tp", scatter_dimension=1, tiled=True).astype(jnp.bfloat16)
    return (mixed, hessian)


STAGE = 512
WIDE = 256
PAIR = 2 * GROUP


def pieces(total, parts):
    parts = min(parts, total)
    counts = [total // parts + (1 if i < total % parts else 0) for i in range(parts)]
    return [(sum(counts[:i]), counts[i]) for i in range(parts)]


def moe_kernel(
    plan,
    tokens,
    routes,
    route_weights,
    gate_codes,
    gate_scales,
    up_codes,
    up_scales,
    down_codes,
    down_scales,
    mixed,
    hidden_out,
    gate_v,
    up_v,
    down_v,
    gate_s,
    up_s,
    down_s,
    gate_acc,
    up_acc,
    lhs,
    lhs_down,
    *rest,
):
    ep_size, slots, out_parts, back_parts = plan
    nd, nb = len(out_parts), len(back_parts)
    sends, recvs = rest[:nd], rest[nd : 2 * nd]
    psends, precvs = rest[2 * nd : 2 * nd + nb], rest[2 * nd + nb : 2 * nd + 2 * nb]
    scale_sem, gate_sem, up_sem, down_sem, out_send, out_recv, back_send, back_recv = rest[2 * nd + 2 * nb :]
    me = lax.axis_index("ep")
    width, units = gate_v.shape
    rows = ep_size * slots
    toks = tokens.shape[0]
    stages = width // STAGE
    downs = down_v.shape[1] // STAGE

    def peer(off):
        return {"ep": lax.rem(me + off, ep_size)}

    barrier = pltpu.get_barrier_semaphore()
    for off in range(1, ep_size):
        pl.semaphore_signal(barrier, inc=1, device_id=peer(off), device_id_type=pl.DeviceIdType.MESH)

    scale_loads = [
        pltpu.make_async_copy(gate_scales, gate_s, scale_sem.at[0]),
        pltpu.make_async_copy(up_scales, up_s, scale_sem.at[1]),
        pltpu.make_async_copy(down_scales, down_s, scale_sem.at[2]),
    ]
    gate_loads, up_loads, down_loads = [], [], []
    for st in range(stages):
        part = pl.ds(st * STAGE, STAGE)
        gate_loads.append(pltpu.make_async_copy(gate_codes.at[part], gate_v.at[part], gate_sem.at[st]))
        up_loads.append(pltpu.make_async_copy(up_codes.at[part], up_v.at[part], up_sem.at[st]))
    for st in range(downs):
        part = pl.ds(st * STAGE, STAGE)
        down_loads.append(pltpu.make_async_copy(down_codes.at[:, part], down_v.at[:, part], down_sem.at[st]))
    scale_loads[0].start()
    scale_loads[1].start()
    for st in range(stages):
        gate_loads[st].start()
        up_loads[st].start()
    scale_loads[2].start()
    for load in down_loads:
        load.start()

    row = lax.broadcasted_iota(jnp.int32, (rows, routes.shape[1]), 0)
    expert = lax.rem(me + row // slots, ep_size)
    slot = (row - (row // slots) * slots)[:, :1].astype(jnp.float32)
    seen = jnp.zeros((rows, 1), jnp.float32)
    chosen, factors = [], []
    for t in range(toks):
        hit = (routes[t : t + 1, :] == expert).astype(jnp.float32)
        named = jnp.sum(hit, axis=1, keepdims=True)
        take = named * (seen == slot).astype(jnp.float32)
        weight = jnp.sum(hit * route_weights[t : t + 1, :].astype(jnp.float32), axis=1, keepdims=True)
        chosen.append(take)
        factors.append(take * weight)
        seen = seen + named

    for c, (first, count) in enumerate(out_parts):
        for st in range(count):
            lo = (first + st) * STAGE
            value = chosen[0] * tokens[0:1, lo : lo + STAGE].astype(jnp.float32)
            for t in range(1, toks):
                value = value + chosen[t] * tokens[t : t + 1, lo : lo + STAGE].astype(jnp.float32)
            value = value.reshape(ep_size, slots, STAGE).astype(jnp.bfloat16)
            sends[c][:, :, st * STAGE : (st + 1) * STAGE] = value

    pl.semaphore_wait(barrier, ep_size - 1)

    def exchange(source, target, send_sem, recv_sem, c, sign):
        copies = []
        for off in range(1, ep_size):
            copies.append(
                pltpu.make_async_remote_copy(
                    src_ref=source.at[off],
                    dst_ref=target.at[off],
                    send_sem=send_sem.at[c, off],
                    recv_sem=recv_sem.at[c, off],
                    device_id=peer(off if sign > 0 else ep_size - off),
                    device_id_type=pl.DeviceIdType.MESH,
                )
            )
        for copy in copies:
            copy.start()
        return copies

    moves = [exchange(sends[c], recvs[c], out_send, out_recv, c, 1) for c in range(nd)]

    lhs[...] = jnp.zeros_like(lhs)
    lhs_down[...] = jnp.zeros_like(lhs_down)
    scale_loads[0].wait()
    scale_loads[1].wait()

    for c, (first, count) in enumerate(out_parts):
        recvs[c][0] = sends[c][0]
        for copy in moves[c]:
            copy.wait_recv()
        for st in range(first, first + count):
            block = recvs[c][:, :, (st - first) * STAGE : (st - first + 1) * STAGE]
            block = block.astype(jnp.float32).reshape(rows, STAGE).astype(jnp.bfloat16)
            pairs = STAGE // PAIR
            for p in range(pairs):
                lhs[st * pairs + p, :rows, :GROUP] = block[:, p * PAIR : p * PAIR + GROUP]
                lhs[st * pairs + p, rows:, GROUP:] = block[:, p * PAIR + GROUP : (p + 1) * PAIR]
            gate_loads[st].wait()
            up_loads[st].wait()

            def columns(n, _, st=st, pairs=pairs):
                cols = pl.ds(pl.multiple_of(n * WIDE, WIDE), WIDE)
                for codes, scales, acc in ((gate_v, gate_s, gate_acc), (up_v, up_s, up_acc)):
                    total = None if st == 0 else acc[:, cols]
                    for p in range(pairs):
                        at = st * pairs + p
                        got = jnp.dot(
                            lhs[at, :rows, :GROUP], codes[at * PAIR : at * PAIR + GROUP, cols], preferred_element_type=jnp.float32
                        )
                        got2 = jnp.dot(
                            lhs[at, rows:, GROUP:], codes[at * PAIR + GROUP: (at + 1) * PAIR, cols], preferred_element_type=jnp.float32
                        )
                        term = got * scales[2 * at : 2 * at + 1, cols]
                        term = term + got2 * scales[2 * at + 1 : 2 * at + 2, cols]
                        total = term if total is None else total + term
                    acc[:, cols] = total
                return 0

            lax.fori_loop(0, units // WIDE, columns, 0, unroll=4)

    for p in range(units // PAIR):
        gate = gate_acc[:, p * PAIR : (p + 1) * PAIR]
        up = up_acc[:, p * PAIR : (p + 1) * PAIR]
        value = (jax.nn.silu(gate) * up).astype(jnp.bfloat16)
        hidden_out[:, p * PAIR : (p + 1) * PAIR] = value
        lhs_down[p, :rows, :GROUP] = value[:, :GROUP]
        lhs_down[p, rows:, GROUP:] = value[:, GROUP:]

    scale_loads[2].wait()
    backs = []
    for c, (first, count) in enumerate(back_parts):
        for st in range(first, first + count):
            down_loads[st].wait()
            for n in range(STAGE // WIDE):
                lo = st * STAGE + n * WIDE
                total = None
                for at in range(units // PAIR):
                    got = jnp.dot(
                        lhs_down[at, :rows, :GROUP],
                        down_v[at * PAIR : at * PAIR + GROUP, lo : lo + WIDE],
                        preferred_element_type=jnp.float32,
                    )
                    got2 = jnp.dot(
                        lhs_down[at, rows:, GROUP:],
                        down_v[at * PAIR + GROUP: (at + 1) * PAIR, lo : lo + WIDE],
                        preferred_element_type=jnp.float32,
                    )
                    term = got * down_s[2 * at : 2 * at + 1, lo : lo + WIDE]
                    term = term + got2 * down_s[2 * at + 1 : 2 * at + 2, lo : lo + WIDE]
                    total = term if total is None else total + term
                here = lo - first * STAGE
                psends[c][:, :, here : here + WIDE] = total.reshape(ep_size, slots, WIDE).astype(jnp.bfloat16)
        backs.append(exchange(psends[c], precvs[c], back_send, back_recv, c, -1))

    for c, (first, count) in enumerate(back_parts):
        precvs[c][0] = psends[c][0]
        for copy in backs[c]:
            copy.wait_recv()
        for st in range(count):
            value = precvs[c][:, :, st * STAGE : (st + 1) * STAGE].astype(jnp.float32).reshape(rows, STAGE)
            lo = (first + st) * STAGE
            for t in range(toks):
                total = jnp.sum(value * factors[t], axis=0, keepdims=True)
                mixed[t : t + 1, lo : lo + STAGE] = total.astype(jnp.bfloat16)

    for copies in moves + backs:
        for copy in copies:
            copy.wait_send()


def hessian_kernel(factor, hidden, out, held, sem):
    rows = held.shape[0] // sem.shape[0]
    copies = []
    for i in range(sem.shape[0]):
        part = pl.ds(i * rows, rows)
        scaled = (hidden[:, i * rows : (i + 1) * rows].astype(jnp.float32) * factor).astype(jnp.bfloat16)
        held[part] = lax.dot_general(scaled, hidden[...], (((0,), (0,)), ((), ())), preferred_element_type=jnp.float32)
        copies.append(pltpu.make_async_copy(held.at[part], out.at[part], sem.at[i]))
        copies[-1].start()
    for copy in copies:
        copy.wait()


def fused_body(*args):
    tokens, routes, route_weights, gate_codes, gate_scales, up_codes, up_scales, down_codes, down_scales = args
    ep_size = lax.axis_size("ep")
    toks, width = tokens.shape
    units = gate_codes.shape[1]
    slots = toks * routes.shape[1] // ep_size
    rows = ep_size * slots
    out_parts = pieces(width // STAGE, 2)
    back_parts = pieces(width // STAGE, 3)
    nd, nb = len(out_parts), len(back_parts)
    slabs = [pltpu.VMEM((ep_size, slots, count * STAGE), jnp.bfloat16) for _, count in out_parts]
    back_slabs = [pltpu.VMEM((ep_size, slots, count * STAGE), jnp.bfloat16) for _, count in back_parts]
    stages = width // STAGE
    whole = pl.BlockSpec(memory_space=pltpu.VMEM)
    far = pl.BlockSpec(memory_space=pl.ANY)
    mixed, hidden = pl.pallas_call(
        functools.partial(moe_kernel, (ep_size, slots, out_parts, back_parts)),
        out_shape=(
            jax.ShapeDtypeStruct((toks, width), jnp.bfloat16),
            jax.ShapeDtypeStruct((rows, units), jnp.bfloat16),
        ),
        in_specs=[whole] * 3 + [far] * 6,
        out_specs=(whole, whole),
        scratch_shapes=[
            pltpu.VMEM(gate_codes.shape, jnp.bfloat16),
            pltpu.VMEM(up_codes.shape, jnp.bfloat16),
            pltpu.VMEM(down_codes.shape, jnp.bfloat16),
            pltpu.VMEM(gate_scales.shape, jnp.float32),
            pltpu.VMEM(up_scales.shape, jnp.float32),
            pltpu.VMEM(down_scales.shape, jnp.float32),
            pltpu.VMEM((rows, units), jnp.float32),
            pltpu.VMEM((rows, units), jnp.float32),
            pltpu.VMEM((width // PAIR, 2 * rows, PAIR), jnp.bfloat16),
            pltpu.VMEM((units // PAIR, 2 * rows, PAIR), jnp.bfloat16),
            *slabs,
            *slabs,
            *back_slabs,
            *back_slabs,
            pltpu.SemaphoreType.DMA((3,)),
            pltpu.SemaphoreType.DMA((stages,)),
            pltpu.SemaphoreType.DMA((stages,)),
            pltpu.SemaphoreType.DMA((stages,)),
            pltpu.SemaphoreType.DMA((nd, ep_size)),
            pltpu.SemaphoreType.DMA((nd, ep_size)),
            pltpu.SemaphoreType.DMA((nb, ep_size)),
            pltpu.SemaphoreType.DMA((nb, ep_size)),
        ],
        compiler_params=pltpu.CompilerParams(
            collective_id=0, has_side_effects=True, vmem_limit_bytes=58 * 2**20
        ),
        name="moe",
    )(tokens, routes, route_weights, gate_codes, gate_scales, up_codes, up_scales, down_codes, down_scales)
    block = 128
    hessian = pl.pallas_call(
        functools.partial(hessian_kernel, 2.0 / (toks * ep_size)),
        out_shape=jax.ShapeDtypeStruct((units, units), jnp.float32),
        in_specs=[whole],
        out_specs=far,
        scratch_shapes=[pltpu.VMEM((units, units), jnp.float32), pltpu.SemaphoreType.DMA((units // block,))],
        compiler_params=pltpu.CompilerParams(vmem_limit_bytes=32 * 2**20),
        name="hessian",
    )(hidden)
    return (mixed, hessian)


def fits(mesh, tokens, routes, gate_codes, down_codes):
    ep_size = mesh.shape["ep"]
    toks = tokens.shape[0] // (mesh.shape["groups"] * ep_size)
    units = gate_codes.shape[1] // (ep_size * mesh.shape["tp"])
    asked = toks * routes.shape[1]
    rows_limit = min(toks, asked // ep_size + 2 * (toks // 8))
    return (
        mesh.shape["tp"] == 1
        and units == FF
        and asked == ep_size * rows_limit
        and tokens.shape[1] % STAGE == 0
        and units % STAGE == 0
        and math.frexp(toks * ep_size)[0] == 0.5
    )


def solution(mesh):
    placed = (
        P(("groups", "ep"), None),
        P(("groups", "ep"), None),
        P(("groups", "ep"), None),
        P(None, ("ep", "tp")),
        P(None, ("ep", "tp")),
        P(None, ("ep", "tp")),
        P(None, ("ep", "tp")),
        P(("ep", "tp"), None),
        P(("ep", "tp"), None),
    )

    def run(*args):
        fused = fits(mesh, args[0], args[1], args[3], args[7])
        return jax.shard_map(
            fused_body if fused else body,
            mesh=mesh,
            in_specs=placed,
            out_specs=(P(("groups", "ep"), "tp"), P(("groups", "ep", "tp"), None)),
            check_vma=False,
        )(*args)

    return run
```

```python
import functools
import math

import jax
import jax.numpy as jnp
from jax import lax
from jax.experimental import pallas as pl
from jax.experimental.pallas import tpu as pltpu
from jax.sharding import PartitionSpec as P

FF = 2048
GROUP = 128


def dequantize(codes, scales):
    height, across = codes.shape
    blocks = codes.astype(jnp.float32).reshape(height // GROUP, GROUP, across) * scales[:, None, :]
    return blocks.reshape(height, across).astype(jnp.bfloat16)


def slot_targets(flat, experts, capacity):
    table = (flat[..., None] == jnp.arange(experts, dtype=jnp.int32)).astype(jnp.int32)
    earlier = jnp.cumsum(table, axis=-2) - table
    return flat * capacity + jnp.sum(earlier * table, axis=-1)


def pack_rows(tokens, targets, places, choose):
    count = places.shape[0]
    select = (targets[None, :] == places[:, None]).astype(jnp.bfloat16)
    select = select.reshape(count, tokens.shape[0], choose).sum(axis=2)
    return jnp.dot(select, tokens, preferred_element_type=jnp.float32).astype(jnp.bfloat16)


def body(
    tokens,
    routes,
    route_weights,
    gate_codes,
    gate_scales,
    up_codes,
    up_scales,
    down_codes,
    down_scales,
):
    ep_size = lax.axis_size("ep")
    tp_size = lax.axis_size("tp")
    rows, width = tokens.shape
    choose = routes.shape[1]
    unit_count = gate_codes.shape[1]
    sharing = FF // (tp_size * unit_count)
    experts = ep_size // sharing
    capacity = min(rows, rows * choose // experts + 2 * (rows // 8))
    w_gate = dequantize(gate_codes, gate_scales)
    w_up = dequantize(up_codes, up_scales)
    w_down = dequantize(down_codes, down_scales)
    targets = slot_targets(routes.reshape(-1), experts, capacity)
    places = jnp.arange(experts * capacity, dtype=jnp.int32)
    packed = pack_rows(tokens, targets, places, choose).reshape(experts, 1, capacity, width)
    packed = jnp.broadcast_to(packed, (experts, sharing, capacity, width)).reshape(
        ep_size, capacity, width
    )
    arrived = lax.all_to_all(packed, "ep", split_axis=0, concat_axis=0, tiled=True)
    rows_in = arrived.reshape(ep_size * capacity, width)
    gate = jnp.dot(rows_in, w_gate, preferred_element_type=jnp.float32)
    up = jnp.dot(rows_in, w_up, preferred_element_type=jnp.float32)
    hidden = (jax.nn.silu(gate) * up).astype(jnp.bfloat16)
    paired = lax.all_gather(hidden, "tp", axis=1, tiled=True)
    hessian = lax.dot_general(
        hidden, paired, (((0,), (0,)), ((), ())), preferred_element_type=jnp.float32
    ) * (2.0 / (rows * ep_size))
    partial_value = jnp.dot(hidden, w_down, preferred_element_type=jnp.float32).astype(jnp.bfloat16)
    returned = lax.all_to_all(
        partial_value.reshape(ep_size, capacity, width),
        "ep",
        split_axis=0,
        concat_axis=0,
        tiled=True,
    )
    slots = jnp.arange(experts * capacity, dtype=jnp.int32)
    spread = (targets[:, None] == slots[None, :]).astype(jnp.float32) * route_weights.reshape(
        -1
    ).astype(jnp.float32)[:, None]
    spread = (
        spread.reshape(rows, choose, experts * capacity)
        .sum(axis=1)
        .reshape(rows, experts, 1, capacity)
    )
    spread = jnp.broadcast_to(spread, (rows, experts, sharing, capacity)).reshape(
        rows, ep_size * capacity
    )
    combined = jnp.dot(
        spread.astype(jnp.bfloat16),
        returned.reshape(ep_size * capacity, width),
        preferred_element_type=jnp.float32,
    )
    mixed = lax.psum_scatter(combined, "tp", scatter_dimension=1, tiled=True).astype(jnp.bfloat16)
    return (mixed, hessian)


STAGE = 512
WIDE = 256
PAIR = 2 * GROUP


def pieces(total, parts):
    parts = min(parts, total)
    counts = [total // parts + (1 if i < total % parts else 0) for i in range(parts)]
    return [(sum(counts[:i]), counts[i]) for i in range(parts)]


def moe_kernel(
    plan,
    tokens,
    routes,
    route_weights,
    gate_codes,
    gate_scales,
    up_codes,
    up_scales,
    down_codes,
    down_scales,
    mixed,
    hidden_out,
    gate_v,
    up_v,
    down_v,
    gate_s,
    up_s,
    down_s,
    gate_acc,
    up_acc,
    lhs,
    lhs_down,
    *rest,
):
    ep_size, slots, out_parts, back_parts = plan
    nd, nb = len(out_parts), len(back_parts)
    sends, recvs = rest[:nd], rest[nd : 2 * nd]
    psends, precvs = rest[2 * nd : 2 * nd + nb], rest[2 * nd + nb : 2 * nd + 2 * nb]
    scale_sem, gate_sem, up_sem, down_sem, out_send, out_recv, back_send, back_recv = rest[2 * nd + 2 * nb :]
    me = lax.axis_index("ep")
    width, units = gate_v.shape
    rows = ep_size * slots
    toks = tokens.shape[0]
    stages = width // STAGE
    downs = down_v.shape[1] // STAGE

    def peer(off):
        return {"ep": lax.rem(me + off, ep_size)}

    barrier = pltpu.get_barrier_semaphore()
    for off in range(1, ep_size):
        pl.semaphore_signal(barrier, inc=1, device_id=peer(off), device_id_type=pl.DeviceIdType.MESH)

    scale_loads = [
        pltpu.make_async_copy(gate_scales, gate_s, scale_sem.at[0]),
        pltpu.make_async_copy(up_scales, up_s, scale_sem.at[1]),
        pltpu.make_async_copy(down_scales, down_s, scale_sem.at[2]),
    ]
    gate_loads, up_loads, down_loads = [], [], []
    for st in range(stages):
        part = pl.ds(st * STAGE, STAGE)
        gate_loads.append(pltpu.make_async_copy(gate_codes.at[part], gate_v.at[part], gate_sem.at[st]))
        up_loads.append(pltpu.make_async_copy(up_codes.at[part], up_v.at[part], up_sem.at[st]))
    for st in range(downs):
        part = pl.ds(st * STAGE, STAGE)
        down_loads.append(pltpu.make_async_copy(down_codes.at[:, part], down_v.at[:, part], down_sem.at[st]))
    scale_loads[0].start()
    scale_loads[1].start()
    for st in range(stages):
        gate_loads[st].start()
        up_loads[st].start()
    scale_loads[2].start()
    for load in down_loads:
        load.start()

    row = lax.broadcasted_iota(jnp.int32, (rows, routes.shape[1]), 0)
    expert = lax.rem(me + row // slots, ep_size)
    slot = (row - (row // slots) * slots)[:, :1].astype(jnp.float32)
    seen = jnp.zeros((rows, 1), jnp.float32)
    chosen, factors = [], []
    for t in range(toks):
        hit = (routes[t : t + 1, :] == expert).astype(jnp.float32)
        named = jnp.sum(hit, axis=1, keepdims=True)
        take = named * (seen == slot).astype(jnp.float32)
        weight = jnp.sum(hit * route_weights[t : t + 1, :].astype(jnp.float32), axis=1, keepdims=True)
        chosen.append(take)
        factors.append(take * weight)
        seen = seen + named

    for c, (first, count) in enumerate(out_parts):
        for st in range(count):
            lo = (first + st) * STAGE
            value = chosen[0] * tokens[0:1, lo : lo + STAGE].astype(jnp.float32)
            for t in range(1, toks):
                value = value + chosen[t] * tokens[t : t + 1, lo : lo + STAGE].astype(jnp.float32)
            value = value.reshape(ep_size, slots, STAGE).astype(jnp.bfloat16)
            sends[c][:, :, st * STAGE : (st + 1) * STAGE] = value

    pl.semaphore_wait(barrier, ep_size - 1)

    def exchange(source, target, send_sem, recv_sem, c, sign):
        copies = []
        for off in range(1, ep_size):
            copies.append(
                pltpu.make_async_remote_copy(
                    src_ref=source.at[off],
                    dst_ref=target.at[off],
                    send_sem=send_sem.at[c, off],
                    recv_sem=recv_sem.at[c, off],
                    device_id=peer(off if sign > 0 else ep_size - off),
                    device_id_type=pl.DeviceIdType.MESH,
                )
            )
        for copy in copies:
            copy.start()
        return copies

    moves = [exchange(sends[c], recvs[c], out_send, out_recv, c, 1) for c in range(nd)]

    scale_loads[0].wait()
    scale_loads[1].wait()

    for c, (first, count) in enumerate(out_parts):
        recvs[c][0] = sends[c][0]
        for copy in moves[c]:
            copy.wait_recv()
        for st in range(first, first + count):
            block = recvs[c][:, :, (st - first) * STAGE : (st - first + 1) * STAGE]
            block = block.astype(jnp.float32).reshape(rows, STAGE).astype(jnp.bfloat16)
            pairs = STAGE // PAIR
            for p in range(pairs):
                lhs[st * pairs + p, :rows, :GROUP] = block[:, p * PAIR : p * PAIR + GROUP]
                lhs[st * pairs + p, rows:, GROUP:] = block[:, p * PAIR + GROUP : (p + 1) * PAIR]
            gate_loads[st].wait()
            up_loads[st].wait()

            def columns(n, _, st=st, pairs=pairs):
                cols = pl.ds(pl.multiple_of(n * WIDE, WIDE), WIDE)
                for codes, scales, acc in ((gate_v, gate_s, gate_acc), (up_v, up_s, up_acc)):
                    total = None if st == 0 else acc[:, cols]
                    for p in range(pairs):
                        at = st * pairs + p
                        got = jnp.dot(
                            lhs[at, :rows, :GROUP], codes[at * PAIR : at * PAIR + GROUP, cols], preferred_element_type=jnp.float32
                        )
                        got2 = jnp.dot(
                            lhs[at, rows:, GROUP:], codes[at * PAIR + GROUP: (at + 1) * PAIR, cols], preferred_element_type=jnp.float32
                        )
                        term = got * scales[2 * at : 2 * at + 1, cols]
                        term = term + got2 * scales[2 * at + 1 : 2 * at + 2, cols]
                        total = term if total is None else total + term
                    acc[:, cols] = total
                return 0

            lax.fori_loop(0, units // WIDE, columns, 0, unroll=4)

    for p in range(units // PAIR):
        gate = gate_acc[:, p * PAIR : (p + 1) * PAIR]
        up = up_acc[:, p * PAIR : (p + 1) * PAIR]
        value = (jax.nn.silu(gate) * up).astype(jnp.bfloat16)
        hidden_out[:, p * PAIR : (p + 1) * PAIR] = value
        lhs_down[p, :rows, :GROUP] = value[:, :GROUP]
        lhs_down[p, rows:, GROUP:] = value[:, GROUP:]

    scale_loads[2].wait()
    backs = []
    for c, (first, count) in enumerate(back_parts):
        for st in range(first, first + count):
            down_loads[st].wait()
            for n in range(STAGE // WIDE):
                lo = st * STAGE + n * WIDE
                total = None
                for at in range(units // PAIR):
                    got = jnp.dot(
                        lhs_down[at, :rows, :GROUP],
                        down_v[at * PAIR : at * PAIR + GROUP, lo : lo + WIDE],
                        preferred_element_type=jnp.float32,
                    )
                    got2 = jnp.dot(
                        lhs_down[at, rows:, GROUP:],
                        down_v[at * PAIR + GROUP: (at + 1) * PAIR, lo : lo + WIDE],
                        preferred_element_type=jnp.float32,
                    )
                    term = got * down_s[2 * at : 2 * at + 1, lo : lo + WIDE]
                    term = term + got2 * down_s[2 * at + 1 : 2 * at + 2, lo : lo + WIDE]
                    total = term if total is None else total + term
                here = lo - first * STAGE
                psends[c][:, :, here : here + WIDE] = total.reshape(ep_size, slots, WIDE).astype(jnp.bfloat16)
        backs.append(exchange(psends[c], precvs[c], back_send, back_recv, c, -1))

    for c, (first, count) in enumerate(back_parts):
        precvs[c][0] = psends[c][0]
        for copy in backs[c]:
            copy.wait_recv()
        for st in range(count):
            value = precvs[c][:, :, st * STAGE : (st + 1) * STAGE].astype(jnp.float32).reshape(rows, STAGE)
            lo = (first + st) * STAGE
            for t in range(toks):
                total = jnp.sum(value * factors[t], axis=0, keepdims=True)
                mixed[t : t + 1, lo : lo + STAGE] = total.astype(jnp.bfloat16)

    for copies in moves + backs:
        for copy in copies:
            copy.wait_send()


def hessian_kernel(factor, hidden, out, held, sem):
    rows = held.shape[0] // sem.shape[0]
    copies = []
    for i in range(sem.shape[0]):
        part = pl.ds(i * rows, rows)
        scaled = (hidden[:, i * rows : (i + 1) * rows].astype(jnp.float32) * factor).astype(jnp.bfloat16)
        held[part] = lax.dot_general(scaled, hidden[...], (((0,), (0,)), ((), ())), preferred_element_type=jnp.float32)
        copies.append(pltpu.make_async_copy(held.at[part], out.at[part], sem.at[i]))
        copies[-1].start()
    for copy in copies:
        copy.wait()


def fused_body(*args):
    tokens, routes, route_weights, gate_codes, gate_scales, up_codes, up_scales, down_codes, down_scales = args
    ep_size = lax.axis_size("ep")
    toks, width = tokens.shape
    units = gate_codes.shape[1]
    slots = toks * routes.shape[1] // ep_size
    rows = ep_size * slots
    out_parts = pieces(width // STAGE, 1)
    back_parts = pieces(width // STAGE, 4)
    nd, nb = len(out_parts), len(back_parts)
    slabs = [pltpu.VMEM((ep_size, slots, count * STAGE), jnp.bfloat16) for _, count in out_parts]
    back_slabs = [pltpu.VMEM((ep_size, slots, count * STAGE), jnp.bfloat16) for _, count in back_parts]
    stages = width // STAGE
    whole = pl.BlockSpec(memory_space=pltpu.VMEM)
    far = pl.BlockSpec(memory_space=pl.ANY)
    mixed, hidden = pl.pallas_call(
        functools.partial(moe_kernel, (ep_size, slots, out_parts, back_parts)),
        out_shape=(
            jax.ShapeDtypeStruct((toks, width), jnp.bfloat16),
            jax.ShapeDtypeStruct((rows, units), jnp.bfloat16),
        ),
        in_specs=[whole] * 3 + [far] * 6,
        out_specs=(whole, whole),
        scratch_shapes=[
            pltpu.VMEM(gate_codes.shape, jnp.bfloat16),
            pltpu.VMEM(up_codes.shape, jnp.bfloat16),
            pltpu.VMEM(down_codes.shape, jnp.bfloat16),
            pltpu.VMEM(gate_scales.shape, jnp.float32),
            pltpu.VMEM(up_scales.shape, jnp.float32),
            pltpu.VMEM(down_scales.shape, jnp.float32),
            pltpu.VMEM((rows, units), jnp.float32),
            pltpu.VMEM((rows, units), jnp.float32),
            pltpu.VMEM((width // PAIR, 2 * rows, PAIR), jnp.bfloat16),
            pltpu.VMEM((units // PAIR, 2 * rows, PAIR), jnp.bfloat16),
            *slabs,
            *slabs,
            *back_slabs,
            *back_slabs,
            pltpu.SemaphoreType.DMA((3,)),
            pltpu.SemaphoreType.DMA((stages,)),
            pltpu.SemaphoreType.DMA((stages,)),
            pltpu.SemaphoreType.DMA((stages,)),
            pltpu.SemaphoreType.DMA((nd, ep_size)),
            pltpu.SemaphoreType.DMA((nd, ep_size)),
            pltpu.SemaphoreType.DMA((nb, ep_size)),
            pltpu.SemaphoreType.DMA((nb, ep_size)),
        ],
        compiler_params=pltpu.CompilerParams(
            collective_id=0, has_side_effects=True, vmem_limit_bytes=58 * 2**20
        ),
        name="moe",
    )(tokens, routes, route_weights, gate_codes, gate_scales, up_codes, up_scales, down_codes, down_scales)
    block = 128
    hessian = pl.pallas_call(
        functools.partial(hessian_kernel, 2.0 / (toks * ep_size)),
        out_shape=jax.ShapeDtypeStruct((units, units), jnp.float32),
        in_specs=[whole],
        out_specs=far,
        scratch_shapes=[pltpu.VMEM((units, units), jnp.float32), pltpu.SemaphoreType.DMA((units // block,))],
        compiler_params=pltpu.CompilerParams(vmem_limit_bytes=32 * 2**20),
        name="hessian",
    )(hidden)
    return (mixed, hessian)


def fits(mesh, tokens, routes, gate_codes, down_codes):
    ep_size = mesh.shape["ep"]
    toks = tokens.shape[0] // (mesh.shape["groups"] * ep_size)
    units = gate_codes.shape[1] // (ep_size * mesh.shape["tp"])
    asked = toks * routes.shape[1]
    rows_limit = min(toks, asked // ep_size + 2 * (toks // 8))
    return (
        mesh.shape["tp"] == 1
        and units == FF
        and asked == ep_size * rows_limit
        and tokens.shape[1] % STAGE == 0
        and units % STAGE == 0
        and math.frexp(toks * ep_size)[0] == 0.5
    )


def solution(mesh):
    placed = (
        P(("groups", "ep"), None),
        P(("groups", "ep"), None),
        P(("groups", "ep"), None),
        P(None, ("ep", "tp")),
        P(None, ("ep", "tp")),
        P(None, ("ep", "tp")),
        P(None, ("ep", "tp")),
        P(("ep", "tp"), None),
        P(("ep", "tp"), None),
    )

    def run(*args):
        fused = fits(mesh, args[0], args[1], args[3], args[7])
        return jax.shard_map(
            fused_body if fused else body,
            mesh=mesh,
            in_specs=placed,
            out_specs=(P(("groups", "ep"), "tp"), P(("groups", "ep", "tp"), None)),
            check_vma=False,
        )(*args)

    return run
```
